32 devices in a mesh: view: 4 (over z), slab: 8 (over y, x, core).
Axes of the slice: x: 2, y: 2, z: 4, core: 2. Of those that a mesh axis runs over, the one named last changes fastest.
Arguments:
- estimate: float32 [256, 32, 128], P('slab'), may hold values from 0.5 to 2
- recorded: float32 [8, 256, 32, 128], P('view', 'slab'), may hold values from 0.5 to 2
- psf_taps: float32 [8, 3, 31], P('view'), may hold values from 0.02 to 1
- tile_map: int32 [8, 8, 8], P('view'), may hold values from 0 to 63, as said below
Outputs:
- new_estimate: float32 [256, 32, 128], P('slab')
The draws below stay inside these ranges and needn't reach their ends.
Inputs may be any that keep to these rules, and one draw needn't show every extreme that they name: For each view, tile_map[v] is a bijection of the 64 tiles. Each view slab a takes its 8 tiles from the world slabs thus: 2 tiles from world slab a itself, none from exactly one other, one from each of the rest.
All inputs are finite; a program needn't handle non-finite values.
Results may differ from the reference program's by a relative error of at most 0.0003.
Values sent between devices are 32-bit elements; how exact they have to be, the bound alone decides.
A program may use at most 128 MiB of HBM per device.

```python
import math
import jax
import jax.numpy as jnp
from jax import lax

TAPS = 31
ZD = 32
YT = 4
NX = 128
GRID = 8
NZ = 256
NY = 32
VIEWS = 8


def one_view_map(key):
    grid_size = GRID
    keys = jax.random.split(key, 4)
    sigma = jnp.arange(grid_size, dtype=jnp.int32)
    offset = jax.random.randint(keys[1], (), 1, grid_size)
    sigma_other = (jnp.arange(grid_size, dtype=jnp.int32) + offset) % grid_size
    base = jnp.tile(jnp.arange(grid_size, dtype=jnp.int32)[None, :], (grid_size, 1))
    row_lists = jnp.where(base == sigma_other[:, None], sigma[:, None], base)
    row_orders = jax.vmap(lambda sub_key: jax.random.permutation(sub_key, grid_size))(jax.random.split(keys[2], grid_size))
    sources = jnp.take_along_axis(row_lists, row_orders, axis=1).reshape(-1)
    onehot = (sources[:, None] == jnp.arange(grid_size)[None, :]).astype(jnp.int32)
    before = jnp.cumsum(onehot, axis=0) - onehot
    order_rank = jnp.sum(before * onehot, axis=1)
    tile_orders = jax.vmap(lambda sub_key: jax.random.permutation(sub_key, grid_size))(jax.random.split(keys[3], grid_size))
    tiles = tile_orders[sources, order_rank]
    return (sources * grid_size + tiles).reshape(grid_size, grid_size).astype(jnp.int32)


def draw_tile_map(key, part):
    return jax.vmap(one_view_map)(jax.random.split(jax.random.fold_in(key, 17), VIEWS))


def draw_psf_taps(key, part):
    sub_keys = jax.random.split(jax.random.fold_in(key, 29), 3)
    tap_shape = (VIEWS, 3, TAPS)
    wing_taps = jnp.exp(jax.random.uniform(sub_keys[0], tap_shape, jnp.float32, math.log(0.02), math.log(0.1)))
    lobe_taps = jax.random.uniform(sub_keys[1], tap_shape, jnp.float32, 0.5, 1.0)
    lobe_mask = jax.random.bernoulli(sub_keys[2], 0.12, tap_shape)
    centre_tap = lax.broadcasted_iota(jnp.int32, tap_shape, 2) == TAPS // 2
    tap_values = jnp.where(centre_tap, 1.0, jnp.where(lobe_mask, lobe_taps, wing_taps))
    return jnp.clip(tap_values, 0.02, 1.0).astype(jnp.float32)


def levels(own_key, shape, shards, least, top_value):
    factor_of = 1.0
    for axis_at, parts in shards:
        heights = jax.random.uniform(jax.random.fold_in(jax.random.fold_in(own_key, 6), axis_at), (parts,), jnp.float32, least / len(shards), top_value / len(shards))
        factor_of = factor_of * jnp.repeat(jnp.exp(heights), shape[axis_at] // parts).reshape((-1,) + (1,) * (len(shape) - 1 - axis_at))
    return factor_of


def setup_inputs(seed: int = 0) -> dict:
    seeds = jax.random.split(jax.random.key(seed), 5)
    return {
        "estimate": jnp.clip(jnp.exp(math.log(2.0) - 1.3862944 * jax.random.uniform(seeds[0], (NZ, NY, NX), jnp.float32) ** levels(seeds[0], (NZ, NY, NX), ((0, 8),), -0.2, 0.2)), 0.5, 2.0),
        "recorded": jnp.clip(jnp.exp(math.log(2.0) - 1.3862944 * jax.random.uniform(seeds[1], (VIEWS, NZ, NY, NX), jnp.float32) ** levels(seeds[1], (VIEWS, NZ, NY, NX), ((0, 4), (1, 8)), -0.2, 0.2)), 0.5, 2.0),
        "psf_taps": draw_psf_taps(jax.random.fold_in(seeds[4], 71), 0),
        "tile_map": draw_tile_map(jax.random.fold_in(seeds[4], 71), 0),
    }


def blur_axis(volume, weights, axis_number, adjoint):
    moved_volume = jnp.moveaxis(volume, axis_number, 0)
    length = moved_volume.shape[0]
    tap_count = weights.shape[0]
    half_width = tap_count // 2
    padded_ones = jnp.pad(jnp.ones((length,), jnp.float32), half_width)
    divisor = weights[0] * padded_ones[0:length]
    for tap_index in range(1, tap_count):
        divisor = divisor + weights[tap_index] * padded_ones[tap_index:tap_index + length]
    if adjoint:
        moved_volume = moved_volume / divisor[:, None, None]
    padded = jnp.pad(moved_volume, ((half_width, half_width), (0, 0), (0, 0)))
    summed = jnp.zeros_like(moved_volume)
    for tap_index in range(tap_count):
        if adjoint:
            offset = 2 * half_width - tap_index
        else:
            offset = tap_index
        summed = summed + weights[tap_index] * padded[offset:offset + length]
    if not adjoint:
        summed = summed / divisor[:, None, None]
    return jnp.moveaxis(summed, 0, axis_number)


def to_tiles(volume):
    shaped = volume.reshape(GRID, ZD, GRID, YT, NX).transpose(0, 2, 1, 3, 4)
    return shaped.reshape(GRID * GRID, ZD, YT, NX)


def from_tiles(tiles):
    shaped = tiles.reshape(GRID, GRID, ZD, YT, NX).transpose(0, 2, 1, 3, 4)
    return shaped.reshape(NZ, NY, NX)


def reference(estimate, recorded, psf_taps, tile_map):
    world_tiles = to_tiles(estimate)

    def one_view(product, inputs):
        observed, view_taps, view_map = inputs
        weights = view_taps / jnp.sum(view_taps, axis=1, keepdims=True)
        flat_map = view_map.reshape(-1).astype(jnp.int32)
        viewed = from_tiles(world_tiles[flat_map])
        blurred = viewed
        for axis_number in range(3):
            blurred = blur_axis(blurred, weights[axis_number], axis_number, False)
        adjoint_volume = observed / blurred
        for axis_number in range(3):
            adjoint_volume = blur_axis(adjoint_volume, weights[axis_number], axis_number, True)
        placed = jnp.zeros_like(world_tiles).at[flat_map].set(to_tiles(adjoint_volume))
        return product * from_tiles(placed), None

    product, unused = lax.scan(one_view, jnp.ones_like(estimate), (recorded, psf_taps, tile_map))
    return estimate * product
```

```python
import functools

import jax
import jax.numpy as jnp
from jax import lax
from jax.experimental import pallas as pl
from jax.experimental.pallas import tpu as pltpu
from jax.sharding import PartitionSpec as P

HALO = 16
MESH = pl.DeviceIdType.MESH
F32 = jnp.float32
BF16 = jnp.bfloat16


def split(value):
    high = value.astype(BF16)
    low = (value - high.astype(F32)).astype(BF16)
    return high, low


def stacked(value, axis):
    high, low = split(value)
    return jnp.concatenate([high, low, high], axis=axis)


def dot(left, right):
    return jnp.dot(left, right, preferred_element_type=F32)


def select_taps(position, tap, taps):
    total = jnp.zeros(position.shape, F32)
    for t in range(taps):
        total = jnp.where(position == t, tap(t), total)
    return total


def column_divisor(columns, tap, taps, length):
    half = taps // 2
    total = jnp.zeros(columns.shape, F32)
    for t in range(taps):
        cell = columns + (t - half)
        total = total + jnp.where((cell >= 0) & (cell < length), tap(t), 0.0)
    return total


def kernel(n, m, views, taps, *refs):
    table, tap_ref, est_ref, rec_ref, out_ref = refs[:5]
    rest = list(refs[5:])
    height, depth, width = rec_ref.shape[2], rec_ref.shape[1], rec_ref.shape[3]
    tile = height // n
    padded = depth + 2 * HALO
    half = taps // 2
    view = lax.axis_index("view")
    own = lax.axis_index("slab")
    est_t = rest.pop(0)
    send = rest.pop(0)
    arrived = [rest.pop(0) for _ in range(views)]
    pad1 = [rest.pop(0) for _ in range(views)]
    pad2 = [rest.pop(0) for _ in range(views)]
    work = [rest.pop(0) for _ in range(views)]
    back = [[rest.pop(0) for _ in range(tile)] for _ in range(views)]
    up_in, up_out, down_in, down_out = [rest.pop(0) for _ in range(4)]
    lz, lza, ly, lya, rx, rxa = [rest.pop(0) for _ in range(6)]
    f_send, f_recv, h_send, h_recv, b_send, b_recv, c_send, c_recv = rest

    barrier = pltpu.get_barrier_semaphore()

    for v in range(views):
        for pad in (pad1[v], pad2[v]):
            pad[:, 0:HALO, :] = jnp.zeros((height, HALO, width), F32)
            pad[:, HALO + depth:, :] = jnp.zeros((height, HALO, width), F32)

    for r in range(1, n):
        pl.semaphore_signal(barrier, inc=1, device_id=(view, lax.rem(own + r, n)), device_id_type=MESH)
    for r in range(1, m):
        pl.semaphore_signal(barrier, inc=1, device_id=(lax.rem(view + r, m), own), device_id_type=MESH)

    for g in range(height // 8):
        block = jnp.swapaxes(est_ref[:, g * 8:g * 8 + 8, :], 0, 1)
        if tile <= 8:
            per = 8 // tile
            est_t[g * per:(g + 1) * per] = block.reshape(per, tile, depth, width)

    pl.semaphore_wait(barrier, n - 1 + m - 1)

    def forward_copy(v, r):
        return pltpu.make_async_remote_copy(
            src_ref=send.at[v, r], dst_ref=arrived[v].at[r],
            send_sem=f_send.at[v, r], recv_sem=f_recv.at[v, r],
            device_id=(view, lax.rem(own + r, n)), device_id_type=MESH)

    for v in range(views):
        for r in range(1, n):
            send[v, r] = est_t[table[v, 0, r]]
            forward_copy(v, r).start()

    for v in range(views):
        for axis in range(3):
            tap = lambda t, v=v, axis=axis: tap_ref[v, axis, t]
            if axis < 2:
                rows, cols, shift, length, start = (
                    (depth, padded, HALO, depth * n, own * depth) if axis == 0 else (height, height, 0, height, 0))
                shape = (rows, 3 * cols)
                row = start + lax.broadcasted_iota(jnp.int32, shape, 0)
                flat = lax.broadcasted_iota(jnp.int32, shape, 1)
                group = (flat >= cols).astype(jnp.int32) + (flat >= 2 * cols).astype(jnp.int32)
                col = start + flat - group * cols - shift
                inside = (col >= 0) & (col < length)
                f = jnp.where(inside, select_taps(col - row + half, tap, taps), 0.0)
                f = f / jnp.sum(jnp.where(group == 0, f, 0.0), axis=1, keepdims=True)
                div = column_divisor(col[0:8], tap, taps, length)[0:1]
                a = jnp.where(inside, select_taps(row - col + half, tap, taps), 0.0)
                a = a / jnp.where(inside[0:1], div, 1.0)
                for ref, value in (((lz, lza), (ly, lya))[axis][0], f), (((lz, lza), (ly, lya))[axis][1], a):
                    high, low = split(value)
                    ref[v] = jnp.where(group == 2, low.astype(F32), high.astype(F32)).astype(BF16)
            else:
                shape = (width, width)
                row = lax.broadcasted_iota(jnp.int32, shape, 0)
                col = lax.broadcasted_iota(jnp.int32, shape, 1)
                f = select_taps(col - row + half, tap, taps)
                f = f / jnp.sum(f, axis=1, keepdims=True)
                a = select_taps(row - col + half, tap, taps)
                a = a / column_divisor(col[0:8], tap, taps, width)[0:1]
                for ref, value in ((rx, a), (rxa, f)):
                    high, low = split(value)
                    ref[v, 0:width] = high
                    ref[v, width:2 * width] = high
                    ref[v, 2 * width:] = low

    has_low, has_high = own > 0, own < n - 1

    def halo_copies(pads, stage, v):
        low = pltpu.make_async_remote_copy(
            src_ref=pads[v].at[:, HALO:2 * HALO, :], dst_ref=pads[v].at[:, HALO + depth:2 * HALO + depth, :],
            send_sem=h_send.at[stage, v, 0], recv_sem=h_recv.at[stage, v, 0],
            device_id=(view, lax.rem(own + n - 1, n)), device_id_type=MESH)
        high = pltpu.make_async_remote_copy(
            src_ref=pads[v].at[:, depth:depth + HALO, :], dst_ref=pads[v].at[:, 0:HALO, :],
            send_sem=h_send.at[stage, v, 1], recv_sem=h_recv.at[stage, v, 1],
            device_id=(view, lax.rem(own + 1, n)), device_id_type=MESH)
        return low, high

    def halo_start(pads, stage, v):
        low, high = halo_copies(pads, stage, v)

        @pl.when(has_low)
        def _():
            low.start()

        @pl.when(has_high)
        def _():
            high.start()

    def halo_wait(pads, stage, v):
        low, high = halo_copies(pads, stage, v)

        @pl.when(has_low)
        def _():
            low.wait_send()
            high.wait_recv()

        @pl.when(has_high)
        def _():
            high.wait_send()
            low.wait_recv()

    def assemble(v):
        for r in range(1, n):
            forward_copy(v, r).wait()
        for c in range(n):
            slot = table[v, 1, c]
            value = jnp.where(slot == 0, est_t[table[v, 2, c]], arrived[v][slot])
            pad1[v][c * tile:(c + 1) * tile, HALO:HALO + depth, :] = value
        halo_start(pad1, 0, v)

    def blur_and_ratio(v):
        halo_wait(pad1, 0, v)

        def first(g, carry):
            left, right = lz[v], rx[v]
            rows = [dot(left, stacked(pad1[v][g * 4 + k], 0)) for k in range(4)]
            value = dot(stacked(jnp.concatenate(rows, axis=0), 1), right)
            work[v][pl.ds(g * 4, 4)] = value.reshape(4, depth, width)
            return carry

        lax.fori_loop(0, height // 4, first, 0)

        def second(g, carry):
            base = pl.multiple_of(g * 8, 8)
            left, left_a, right = ly[v], lya[v], rxa[v]
            block = jnp.swapaxes(work[v][:, pl.ds(base, 8), :], 0, 1)
            rows = []
            for k in range(8):
                blurred = dot(left, stacked(block[k], 0))
                ratio = rec_ref[v, base + k] / blurred
                rows.append(dot(left_a, stacked(ratio, 0)))
            value = dot(stacked(jnp.concatenate(rows, axis=0), 1), right)
            value = jnp.swapaxes(value.reshape(8, height, width), 0, 1)
            pad2[v][:, pl.ds(pl.multiple_of(base + HALO, 8), 8), :] = value
            return carry

        lax.fori_loop(0, depth // 8, second, 0)
        halo_start(pad2, 1, v)

    def back_copy(v, r, q):
        return pltpu.make_async_remote_copy(
            src_ref=send.at[v, r, q], dst_ref=back[v][q].at[r],
            send_sem=b_send.at[v, r, q], recv_sem=b_recv.at[v, r, q],
            device_id=(view, lax.rem(own + r, n)), device_id_type=MESH)

    def finish(v):
        halo_wait(pad2, 1, v)
        for q in range(tile):
            def last(c, carry):
                work[v][c * tile + q] = dot(lza[v], stacked(pad2[v][c * tile + q], 0))
                return carry

            lax.fori_loop(0, n, last, 0, unroll=4)
            for r in range(1, n):
                send[v, r, q] = work[v][table[v, 3, r] * tile + q]
                back_copy(v, r, q).start()

    for v in range(views):
        assemble(v)
    for v in range(views):
        blur_and_ratio(v)
    for v in range(views):
        finish(v)

    has_below, has_above = view > 0, view < m - 1

    def up_copy(q):
        return pltpu.make_async_remote_copy(
            src_ref=up_out.at[q], dst_ref=up_in.at[q], send_sem=c_send.at[0, q], recv_sem=c_recv.at[0, q],
            device_id=(lax.rem(view + 1, m), own), device_id_type=MESH)

    def down_copy(q):
        return pltpu.make_async_remote_copy(
            src_ref=down_out.at[q], dst_ref=down_in.at[q], send_sem=c_send.at[1, q], recv_sem=c_recv.at[1, q],
            device_id=(lax.rem(view + m - 1, m), own), device_id_type=MESH)

    def local_product(q):
        for v in range(views):
            for r in range(1, n):
                back_copy(v, r, q).wait()
        for k in range(n):
            product = None
            for v in range(views):
                slot = table[v, 4, k]
                value = jnp.where(slot == 0, work[v][table[v, 5, k] * tile + q], back[v][q][slot])
                product = value if product is None else product * value
            out_ref[q, k] = product

        @pl.when(view == 0)
        def _():
            up_out[q] = out_ref[q]
            up_copy(q).start()

        @pl.when(view == m - 1)
        def _():
            down_out[q] = out_ref[q]
            down_copy(q).start()

    def relay(q):
        @pl.when(has_below & has_above)
        def _():
            up_copy(q).wait_recv()
            up_out[q] = up_in[q] * out_ref[q]
            up_copy(q).start()
            down_copy(q).wait_recv()
            down_out[q] = down_in[q] * out_ref[q]
            down_copy(q).start()
            out_ref[q] = up_out[q] * down_in[q]

        @pl.when(has_below & jnp.logical_not(has_above))
        def _():
            up_copy(q).wait_recv()
            out_ref[q] = up_in[q] * out_ref[q]

        @pl.when(has_above & jnp.logical_not(has_below))
        def _():
            down_copy(q).wait_recv()
            out_ref[q] = out_ref[q] * down_in[q]

    for q in range(tile):
        local_product(q)
        if q > 0:
            relay(q - 1)
    relay(tile - 1)
    for q in range(tile):
        @pl.when(has_above)
        def _():
            up_copy(q).wait_send()

        @pl.when(has_below)
        def _():
            down_copy(q).wait_send()


def local(n, m, estimate, recorded, psf_taps, tile_map):
    views, _, taps = psf_taps.shape
    depth, height, width = estimate.shape
    tile = height // n
    own = lax.axis_index("slab")
    count = jnp.arange(n, dtype=jnp.int32)
    flat = tile_map.reshape(views, 1, n * n)
    where_shown = (flat == (own * n + count)[None, :, None]).astype(jnp.int32)
    inverse = jnp.sum(where_shown * jnp.arange(n * n, dtype=jnp.int32), axis=2)
    shown = lax.dynamic_index_in_dim(tile_map, own, 1, keepdims=False)

    def choose(slabs):
        ahead = (slabs - own + n) % n
        hits = (ahead[:, None, :] == count[None, :, None]) & (count[None, :, None] > 0)
        return jnp.sum(hits.astype(jnp.int32) * count, axis=2)

    table = jnp.stack(
        [choose(inverse // n), (own - shown // n + n) % n, shown % n,
         choose(shown // n), (own - inverse // n + n) % n, inverse % n], axis=1)

    padded = depth + 2 * HALO
    vmem = pltpu.VMEM
    dma = pltpu.SemaphoreType.DMA
    scratch = [vmem((n, tile, depth, width), F32), vmem((views, n, tile, depth, width), F32)]
    scratch += [vmem((n, tile, depth, width), F32) for _ in range(views)]
    scratch += [vmem((height, padded, width), F32) for _ in range(2 * views)]
    scratch += [vmem((height, depth, width), F32) for _ in range(views)]
    scratch += [vmem((n, depth, width), F32) for _ in range(views * tile)]
    scratch += [vmem((tile, n, depth, width), F32) for _ in range(4)]
    scratch += [vmem((views, depth, 3 * padded), BF16) for _ in range(2)]
    scratch += [vmem((views, height, 3 * height), BF16) for _ in range(2)]
    scratch += [vmem((views, 3 * width, width), BF16) for _ in range(2)]
    scratch += [dma((views, n)), dma((views, n)), dma((2, views, 2)), dma((2, views, 2)),
                dma((views, n, tile)), dma((views, n, tile)), dma((2, tile)), dma((2, tile))]
    product = pl.pallas_call(
        functools.partial(kernel, n, m, views, taps),
        out_shape=jax.ShapeDtypeStruct((tile, n, depth, width), F32),
        in_specs=[pl.BlockSpec(memory_space=pltpu.SMEM)] * 2 + [pl.BlockSpec(memory_space=pltpu.VMEM)] * 2,
        out_specs=pl.BlockSpec(memory_space=pltpu.VMEM),
        scratch_shapes=scratch,
        compiler_params=pltpu.CompilerParams(
            collective_id=0, has_side_effects=True, vmem_limit_bytes=60 * 1024 * 1024),
    )(table, psf_taps, estimate, recorded)
    return estimate * product.transpose(2, 1, 0, 3).reshape(depth, height, width)


def solution(mesh):
    n, m = mesh.shape["slab"], mesh.shape["view"]
    in_specs = (
        P("slab", None, None),
        P("view", "slab", None, None),
        P("view", None, None),
        P("view", None, None),
    )
    return jax.shard_map(
        functools.partial(local, n, m), mesh=mesh, in_specs=in_specs,
        out_specs=P("slab", None, None), check_vma=False)
```

```python
import functools

import jax
import jax.numpy as jnp
from jax import lax
from jax.experimental import pallas as pl
from jax.experimental.pallas import tpu as pltpu
from jax.sharding import PartitionSpec as P

HALO = 16
PARTS = 1
MESH = pl.DeviceIdType.MESH
F32 = jnp.float32
BF16 = jnp.bfloat16


def split(value):
    high = value.astype(BF16)
    low = (value - high.astype(F32)).astype(BF16)
    return high, low


def stacked(value, axis):
    high, low = split(value)
    return jnp.concatenate([high, low, high], axis=axis)


def dot(left, right):
    return jnp.dot(left, right, preferred_element_type=F32)


def select_taps(position, tap, taps):
    total = jnp.zeros(position.shape, F32)
    for t in range(taps):
        total = jnp.where(position == t, tap(t), total)
    return total


def column_divisor(columns, tap, taps, length):
    half = taps // 2
    total = jnp.zeros(columns.shape, F32)
    for t in range(taps):
        cell = columns + (t - half)
        total = total + jnp.where((cell >= 0) & (cell < length), tap(t), 0.0)
    return total


def kernel(n, m, views, taps, *refs):
    table, tap_ref, est_ref, rec_ref, out_ref = refs[:5]
    rest = list(refs[5:])
    height, depth, width = rec_ref.shape[2], rec_ref.shape[1], rec_ref.shape[3]
    tile = height // n
    padded = depth + 2 * HALO
    half = taps // 2
    view = lax.axis_index("view")
    own = lax.axis_index("slab")
    est_t = rest.pop(0)
    send = rest.pop(0)
    arrived = [rest.pop(0) for _ in range(views)]
    pad1 = [rest.pop(0) for _ in range(views)]
    pad2 = [rest.pop(0) for _ in range(views)]
    work = [rest.pop(0) for _ in range(views)]
    back = [[rest.pop(0) for _ in range(tile)] for _ in range(views)]
    up_in, up_out, down_in, down_out = [rest.pop(0) for _ in range(4)]
    lz, lza, ly, lya, rx, rxa = [rest.pop(0) for _ in range(6)]
    f_send, f_recv, h_send, h_recv, b_send, b_recv, c_send, c_recv = rest

    barrier = pltpu.get_barrier_semaphore()

    for v in range(views):
        for pad in (pad1[v], pad2[v]):
            pad[:, 0:HALO, :] = jnp.zeros((height, HALO, width), F32)
            pad[:, HALO + depth:, :] = jnp.zeros((height, HALO, width), F32)

    for r in range(1, n):
        pl.semaphore_signal(barrier, inc=1, device_id=(view, lax.rem(own + r, n)), device_id_type=MESH)
    for r in range(1, m):
        pl.semaphore_signal(barrier, inc=1, device_id=(lax.rem(view + r, m), own), device_id_type=MESH)

    for g in range(height // 8):
        block = jnp.swapaxes(est_ref[:, g * 8:g * 8 + 8, :], 0, 1)
        if tile <= 8:
            per = 8 // tile
            est_t[g * per:(g + 1) * per] = block.reshape(per, tile, depth, width)

    pl.semaphore_wait(barrier, n - 1 + m - 1)

    def forward_copy(v, r):
        return pltpu.make_async_remote_copy(
            src_ref=send.at[v, r], dst_ref=arrived[v].at[r],
            send_sem=f_send.at[v, r], recv_sem=f_recv.at[v, r],
            device_id=(view, lax.rem(own + r, n)), device_id_type=MESH)

    for v in range(views):
        for r in range(1, n):
            send[v, r] = est_t[table[v, 0, r]]
            forward_copy(v, r).start()

    for v in range(views):
        for axis in range(3):
            tap = lambda t, v=v, axis=axis: tap_ref[v, axis, t]
            if axis < 2:
                rows, cols, shift, length, start = (
                    (depth, padded, HALO, depth * n, own * depth) if axis == 0 else (height, height, 0, height, 0))
                shape = (rows, 3 * cols)
                row = start + lax.broadcasted_iota(jnp.int32, shape, 0)
                flat = lax.broadcasted_iota(jnp.int32, shape, 1)
                group = (flat >= cols).astype(jnp.int32) + (flat >= 2 * cols).astype(jnp.int32)
                col = start + flat - group * cols - shift
                inside = (col >= 0) & (col < length)
                f = jnp.where(inside, select_taps(col - row + half, tap, taps), 0.0)
                f = f / jnp.sum(jnp.where(group == 0, f, 0.0), axis=1, keepdims=True)
                div = column_divisor(col[0:8], tap, taps, length)[0:1]
                a = jnp.where(inside, select_taps(row - col + half, tap, taps), 0.0)
                a = a / jnp.where(inside[0:1], div, 1.0)
                for ref, value in (((lz, lza), (ly, lya))[axis][0], f), (((lz, lza), (ly, lya))[axis][1], a):
                    high, low = split(value)
                    ref[v] = jnp.where(group == 2, low.astype(F32), high.astype(F32)).astype(BF16)
            else:
                shape = (width, width)
                row = lax.broadcasted_iota(jnp.int32, shape, 0)
                col = lax.broadcasted_iota(jnp.int32, shape, 1)
                f = select_taps(col - row + half, tap, taps)
                f = f / jnp.sum(f, axis=1, keepdims=True)
                a = select_taps(row - col + half, tap, taps)
                a = a / column_divisor(col[0:8], tap, taps, width)[0:1]
                for ref, value in ((rx, a), (rxa, f)):
                    high, low = split(value)
                    ref[v, 0:width] = high
                    ref[v, width:2 * width] = high
                    ref[v, 2 * width:] = low

    has_low, has_high = own > 0, own < n - 1

    def halo_copies(pads, stage, v):
        low = pltpu.make_async_remote_copy(
            src_ref=pads[v].at[:, HALO:2 * HALO, :], dst_ref=pads[v].at[:, HALO + depth:2 * HALO + depth, :],
            send_sem=h_send.at[stage, v, 0], recv_sem=h_recv.at[stage, v, 0],
            device_id=(view, lax.rem(own + n - 1, n)), device_id_type=MESH)
        high = pltpu.make_async_remote_copy(
            src_ref=pads[v].at[:, depth:depth + HALO, :], dst_ref=pads[v].at[:, 0:HALO, :],
            send_sem=h_send.at[stage, v, 1], recv_sem=h_recv.at[stage, v, 1],
            device_id=(view, lax.rem(own + 1, n)), device_id_type=MESH)
        return low, high

    def halo_start(pads, stage, v):
        low, high = halo_copies(pads, stage, v)

        @pl.when(has_low)
        def _():
            low.start()

        @pl.when(has_high)
        def _():
            high.start()

    def halo_wait(pads, stage, v):
        low, high = halo_copies(pads, stage, v)

        @pl.when(has_low)
        def _():
            low.wait_send()
            high.wait_recv()

        @pl.when(has_high)
        def _():
            high.wait_send()
            low.wait_recv()

    def assemble(v):
        for r in range(1, n):
            forward_copy(v, r).wait()
        for c in range(n):
            slot = table[v, 1, c]
            value = jnp.where(slot == 0, est_t[table[v, 2, c]], arrived[v][slot])
            pad1[v][c * tile:(c + 1) * tile, HALO:HALO + depth, :] = value
        halo_start(pad1, 0, v)

    def blur_and_ratio(v):
        halo_wait(pad1, 0, v)

        def first(g, carry):
            left, right = lz[v], rx[v]
            rows = [dot(left, stacked(pad1[v][g * 4 + k], 0)) for k in range(4)]
            value = dot(stacked(jnp.concatenate(rows, axis=0), 1), right)
            work[v][pl.ds(g * 4, 4)] = value.reshape(4, depth, width)
            return carry

        lax.fori_loop(0, height // 4, first, 0)

        def second(g, carry):
            base = pl.multiple_of(g * 8, 8)
            left, left_a, right = ly[v], lya[v], rxa[v]
            block = jnp.swapaxes(work[v][:, pl.ds(base, 8), :], 0, 1)
            rows = []
            for k in range(8):
                blurred = dot(left, stacked(block[k], 0))
                ratio = rec_ref[v, base + k] / blurred
                rows.append(dot(left_a, stacked(ratio, 0)))
            value = dot(stacked(jnp.concatenate(rows, axis=0), 1), right)
            value = jnp.swapaxes(value.reshape(8, height, width), 0, 1)
            pad2[v][:, pl.ds(pl.multiple_of(base + HALO, 8), 8), :] = value
            return carry

        lax.fori_loop(0, depth // 8, second, 0)
        halo_start(pad2, 1, v)

    def back_copy(v, r, q):
        return pltpu.make_async_remote_copy(
            src_ref=send.at[v, r, q], dst_ref=back[v][q].at[r],
            send_sem=b_send.at[v, r, q], recv_sem=b_recv.at[v, r, q],
            device_id=(view, lax.rem(own + r, n)), device_id_type=MESH)

    def finish(v):
        halo_wait(pad2, 1, v)
        for q in range(tile):
            def last(c, carry):
                work[v][c * tile + q] = dot(lza[v], stacked(pad2[v][c * tile + q], 0))
                return carry

            lax.fori_loop(0, n, last, 0, unroll=4)
            for r in range(1, n):
                send[v, r, q] = work[v][table[v, 3, r] * tile + q]
                back_copy(v, r, q).start()

    for v in range(views):
        assemble(v)
    for v in range(views):
        blur_and_ratio(v)
    for v in range(views):
        finish(v)

    has_below, has_above = view > 0, view < m - 1
    lower = 2 * view < m
    parts = up_in.shape[0] // tile
    share = n // parts
    chunks = tile * parts

    def up_copy(i):
        return pltpu.make_async_remote_copy(
            src_ref=up_out.at[i], dst_ref=up_in.at[i], send_sem=c_send.at[0, i], recv_sem=c_recv.at[0, i],
            device_id=(lax.rem(view + 1, m), own), device_id_type=MESH)

    def down_copy(i):
        return pltpu.make_async_remote_copy(
            src_ref=down_out.at[i], dst_ref=down_in.at[i], send_sem=c_send.at[1, i], recv_sem=c_recv.at[1, i],
            device_id=(lax.rem(view + m - 1, m), own), device_id_type=MESH)

    def local_product(i):
        q, part = i // parts, i % parts
        if part == 0:
            for v in range(views):
                for r in range(1, n):
                    back_copy(v, r, q).wait()
        for k in range(share):
            product = None
            for v in range(views):
                world = part * share + k
                slot = table[v, 4, world]
                value = jnp.where(slot == 0, work[v][table[v, 5, world] * tile + q], back[v][q][slot])
                product = value if product is None else product * value
            out_ref[i, k] = product

        @pl.when(view == 0)
        def _():
            up_out[i] = out_ref[i]
            up_copy(i).start()

        @pl.when(view == m - 1)
        def _():
            down_out[i] = out_ref[i]
            down_copy(i).start()

    def pass_up(i):
        @pl.when(has_below)
        def _():
            up_copy(i).wait_recv()

            @pl.when(has_above)
            def _():
                up_out[i] = up_in[i] * out_ref[i]
                up_copy(i).start()

    def pass_down(i):
        @pl.when(has_above)
        def _():
            down_copy(i).wait_recv()

            @pl.when(has_below)
            def _():
                down_out[i] = down_in[i] * out_ref[i]
                down_copy(i).start()

    def near(i):
        @pl.when(lower)
        def _():
            pass_up(i)

        @pl.when(jnp.logical_not(lower))
        def _():
            pass_down(i)

    def far(i):
        @pl.when(lower)
        def _():
            pass_down(i)

        @pl.when(jnp.logical_not(lower))
        def _():
            pass_up(i)

        @pl.when(has_below & has_above)
        def _():
            out_ref[i] = up_out[i] * down_in[i]

        @pl.when(has_below & jnp.logical_not(has_above))
        def _():
            out_ref[i] = out_ref[i] * up_in[i]

        @pl.when(has_above & jnp.logical_not(has_below))
        def _():
            out_ref[i] = out_ref[i] * down_in[i]

    for i in range(chunks):
        local_product(i)
        if i >= parts:
            near(i - parts)
    for i in range(chunks - parts, chunks):
        near(i)
    for i in range(chunks):
        far(i)
    for i in range(chunks):
        @pl.when(has_above)
        def _(i=i):
            up_copy(i).wait_send()

        @pl.when(has_below)
        def _(i=i):
            down_copy(i).wait_send()


def local(n, m, estimate, recorded, psf_taps, tile_map):
    views, _, taps = psf_taps.shape
    depth, height, width = estimate.shape
    tile = height // n
    own = lax.axis_index("slab")
    count = jnp.arange(n, dtype=jnp.int32)
    flat = tile_map.reshape(views, 1, n * n)
    where_shown = (flat == (own * n + count)[None, :, None]).astype(jnp.int32)
    inverse = jnp.sum(where_shown * jnp.arange(n * n, dtype=jnp.int32), axis=2)
    shown = lax.dynamic_index_in_dim(tile_map, own, 1, keepdims=False)

    def choose(slabs):
        ahead = (slabs - own + n) % n
        hits = (ahead[:, None, :] == count[None, :, None]) & (count[None, :, None] > 0)
        return jnp.sum(hits.astype(jnp.int32) * count, axis=2)

    table = jnp.stack(
        [choose(inverse // n), (own - shown // n + n) % n, shown % n,
         choose(shown // n), (own - inverse // n + n) % n, inverse % n], axis=1)

    padded = depth + 2 * HALO
    vmem = pltpu.VMEM
    dma = pltpu.SemaphoreType.DMA
    scratch = [vmem((n, tile, depth, width), F32), vmem((views, n, tile, depth, width), F32)]
    scratch += [vmem((n, tile, depth, width), F32) for _ in range(views)]
    scratch += [vmem((height, padded, width), F32) for _ in range(2 * views)]
    scratch += [vmem((height, depth, width), F32) for _ in range(views)]
    scratch += [vmem((n, depth, width), F32) for _ in range(views * tile)]
    parts = PARTS if n % PARTS == 0 else 1
    chunks = tile * parts
    scratch += [vmem((chunks, n // parts, depth, width), F32) for _ in range(4)]
    scratch += [vmem((views, depth, 3 * padded), BF16) for _ in range(2)]
    scratch += [vmem((views, height, 3 * height), BF16) for _ in range(2)]
    scratch += [vmem((views, 3 * width, width), BF16) for _ in range(2)]
    scratch += [dma((views, n)), dma((views, n)), dma((2, views, 2)), dma((2, views, 2)),
                dma((views, n, tile)), dma((views, n, tile)), dma((2, chunks)), dma((2, chunks))]
    product = pl.pallas_call(
        functools.partial(kernel, n, m, views, taps),
        out_shape=jax.ShapeDtypeStruct((chunks, n // parts, depth, width), F32),
        in_specs=[pl.BlockSpec(memory_space=pltpu.SMEM)] * 2 + [pl.BlockSpec(memory_space=pltpu.VMEM)] * 2,
        out_specs=pl.BlockSpec(memory_space=pltpu.VMEM),
        scratch_shapes=scratch,
        compiler_params=pltpu.CompilerParams(
            collective_id=0, has_side_effects=True, vmem_limit_bytes=60 * 1024 * 1024),
    )(table, psf_taps, estimate, recorded)
    product = product.reshape(tile, n, depth, width)
    return estimate * product.transpose(2, 1, 0, 3).reshape(depth, height, width)


def solution(mesh):
    n, m = mesh.shape["slab"], mesh.shape["view"]
    in_specs = (
        P("slab", None, None),
        P("view", "slab", None, None),
        P("view", None, None),
        P("view", None, None),
    )
    return jax.shard_map(
        functools.partial(local, n, m), mesh=mesh, in_specs=in_specs,
        out_specs=P("slab", None, None), check_vma=False)
```

```python
import functools

import jax
import jax.numpy as jnp
from jax import lax
from jax.experimental import pallas as pl
from jax.experimental.pallas import tpu as pltpu
from jax.sharding import PartitionSpec as P

HALO = 16
PARTS = 1
MESH = pl.DeviceIdType.MESH
F32 = jnp.float32
BF16 = jnp.bfloat16


def split(value):
    high = value.astype(BF16)
    low = (value - high.astype(F32)).astype(BF16)
    return high, low


def stacked(value, axis):
    high, low = split(value)
    return jnp.concatenate([high, low, high], axis=axis)


def dot(left, right):
    return jnp.dot(left, right, preferred_element_type=F32)


def select_taps(position, tap, taps):
    total = jnp.zeros(position.shape, F32)
    for t in range(taps):
        total = jnp.where(position == t, tap(t), total)
    return total


def column_divisor(columns, tap, taps, length):
    half = taps // 2
    total = jnp.zeros(columns.shape, F32)
    for t in range(taps):
        cell = columns + (t - half)
        total = total + jnp.where((cell >= 0) & (cell < length), tap(t), 0.0)
    return total


def kernel(n, m, views, taps, *refs):
    table, tap_ref, est_ref, rec_ref, out_ref = refs[:5]
    rest = list(refs[5:])
    height, depth, width = rec_ref.shape[2], rec_ref.shape[1], rec_ref.shape[3]
    tile = height // n
    padded = depth + 2 * HALO
    half = taps // 2
    view = lax.axis_index("view")
    own = lax.axis_index("slab")
    est_t = rest.pop(0)
    send = rest.pop(0)
    arrived = [rest.pop(0) for _ in range(views)]
    pad1 = [rest.pop(0) for _ in range(views)]
    pad2 = [rest.pop(0) for _ in range(views)]
    work = [rest.pop(0) for _ in range(views)]
    back = [[rest.pop(0) for _ in range(tile)] for _ in range(views)]
    up_in, up_out, down_in, down_out = [rest.pop(0) for _ in range(4)]
    lz, lza, ly, lya, rx, rxa = [rest.pop(0) for _ in range(6)]
    f_send, f_recv, h_send, h_recv, b_send, b_recv, c_send, c_recv = rest

    barrier = pltpu.get_barrier_semaphore()

    for v in range(views):
        pad1[v][:, 0:HALO, :] = jnp.zeros((height, HALO, width), F32)
        pad1[v][:, HALO + depth:, :] = jnp.zeros((height, HALO, width), F32)
        pad2[v][:, :, 0:HALO, :] = jnp.zeros((n, tile, HALO, width), F32)
        pad2[v][:, :, HALO + depth:, :] = jnp.zeros((n, tile, HALO, width), F32)

    for r in range(1, n):
        pl.semaphore_signal(barrier, inc=1, device_id=(view, lax.rem(own + r, n)), device_id_type=MESH)
    for r in range(1, m):
        pl.semaphore_signal(barrier, inc=1, device_id=(lax.rem(view + r, m), own), device_id_type=MESH)

    for g in range(height // 8):
        block = jnp.swapaxes(est_ref[:, g * 8:g * 8 + 8, :], 0, 1)
        if tile <= 8:
            per = 8 // tile
            est_t[g * per:(g + 1) * per] = block.reshape(per, tile, depth, width)

    pl.semaphore_wait(barrier, n - 1 + m - 1)

    def forward_copy(v, r):
        return pltpu.make_async_remote_copy(
            src_ref=send.at[v, r], dst_ref=arrived[v].at[r],
            send_sem=f_send.at[v, r], recv_sem=f_recv.at[v, r],
            device_id=(view, lax.rem(own + r, n)), device_id_type=MESH)

    for v in range(views):
        for r in range(1, n):
            send[v, r] = est_t[table[v, 0, r]]
            forward_copy(v, r).start()

    for v in range(views):
        for axis in range(3):
            tap = lambda t, v=v, axis=axis: tap_ref[v, axis, t]
            if axis < 2:
                rows, cols, shift, length, start = (
                    (depth, padded, HALO, depth * n, own * depth) if axis == 0 else (height, height, 0, height, 0))
                shape = (rows, 3 * cols)
                row = start + lax.broadcasted_iota(jnp.int32, shape, 0)
                flat = lax.broadcasted_iota(jnp.int32, shape, 1)
                group = (flat >= cols).astype(jnp.int32) + (flat >= 2 * cols).astype(jnp.int32)
                col = start + flat - group * cols - shift
                inside = (col >= 0) & (col < length)
                f = jnp.where(inside, select_taps(col - row + half, tap, taps), 0.0)
                f = f / jnp.sum(jnp.where(group == 0, f, 0.0), axis=1, keepdims=True)
                div = column_divisor(col[0:8], tap, taps, length)[0:1]
                a = jnp.where(inside, select_taps(row - col + half, tap, taps), 0.0)
                a = a / jnp.where(inside[0:1], div, 1.0)
                for ref, value in (((lz, lza), (ly, lya))[axis][0], f), (((lz, lza), (ly, lya))[axis][1], a):
                    high, low = split(value)
                    ref[v] = jnp.where(group == 2, low.astype(F32), high.astype(F32)).astype(BF16)
            else:
                shape = (width, width)
                row = lax.broadcasted_iota(jnp.int32, shape, 0)
                col = lax.broadcasted_iota(jnp.int32, shape, 1)
                f = select_taps(col - row + half, tap, taps)
                f = f / jnp.sum(f, axis=1, keepdims=True)
                a = select_taps(row - col + half, tap, taps)
                a = a / column_divisor(col[0:8], tap, taps, width)[0:1]
                for ref, value in ((rx, a), (rxa, f)):
                    high, low = split(value)
                    ref[v, 0:width] = high
                    ref[v, width:2 * width] = high
                    ref[v, 2 * width:] = low

    has_low, has_high = own > 0, own < n - 1

    def halo_copies(v, q):
        if q is None:
            pad, slot = pad1[v], tile
            own_low, own_high = pad.at[:, HALO:2 * HALO, :], pad.at[:, depth:depth + HALO, :]
            far_high, far_low = pad.at[:, HALO + depth:2 * HALO + depth, :], pad.at[:, 0:HALO, :]
        else:
            pad, slot = pad2[v], q
            own_low, own_high = pad.at[:, q, HALO:2 * HALO, :], pad.at[:, q, depth:depth + HALO, :]
            far_high, far_low = pad.at[:, q, HALO + depth:2 * HALO + depth, :], pad.at[:, q, 0:HALO, :]
        low = pltpu.make_async_remote_copy(
            src_ref=own_low, dst_ref=far_high,
            send_sem=h_send.at[v, slot, 0], recv_sem=h_recv.at[v, slot, 0],
            device_id=(view, lax.rem(own + n - 1, n)), device_id_type=MESH)
        high = pltpu.make_async_remote_copy(
            src_ref=own_high, dst_ref=far_low,
            send_sem=h_send.at[v, slot, 1], recv_sem=h_recv.at[v, slot, 1],
            device_id=(view, lax.rem(own + 1, n)), device_id_type=MESH)
        return low, high

    def halo_start(v, q=None):
        low, high = halo_copies(v, q)

        @pl.when(has_low)
        def _():
            low.start()

        @pl.when(has_high)
        def _():
            high.start()

    def halo_wait(v, q=None):
        low, high = halo_copies(v, q)

        @pl.when(has_low)
        def _():
            low.wait_send()
            high.wait_recv()

        @pl.when(has_high)
        def _():
            high.wait_send()
            low.wait_recv()

    def assemble(v):
        for r in range(1, n):
            forward_copy(v, r).wait()
        for c in range(n):
            slot = table[v, 1, c]
            value = jnp.where(slot == 0, est_t[table[v, 2, c]], arrived[v][slot])
            pad1[v][c * tile:(c + 1) * tile, HALO:HALO + depth, :] = value
        halo_start(v)

    def blur_and_ratio(v):
        halo_wait(v)

        def first(g, carry):
            left, right = lz[v], rx[v]
            rows = [dot(left, stacked(pad1[v][g * 4 + k], 0)) for k in range(4)]
            value = dot(stacked(jnp.concatenate(rows, axis=0), 1), right)
            work[v][pl.ds(g * 4, 4)] = value.reshape(4, depth, width)
            return carry

        lax.fori_loop(0, height // 4, first, 0)

        def second(g, carry):
            base = pl.multiple_of(g * 8, 8)
            left, left_a, right = ly[v], lya[v], rxa[v]
            block = jnp.swapaxes(work[v][:, pl.ds(base, 8), :], 0, 1)
            rows = []
            for k in range(8):
                blurred = dot(left, stacked(block[k], 0))
                ratio = rec_ref[v, base + k] / blurred
                rows.append(dot(left_a, stacked(ratio, 0)))
            value = dot(stacked(jnp.concatenate(rows, axis=0), 1), right)
            value = jnp.swapaxes(value.reshape(8, height, width), 0, 1).reshape(n, tile, 8, width)
            pad2[v][:, :, pl.ds(pl.multiple_of(base + HALO, 8), 8), :] = value
            return carry

        lax.fori_loop(0, depth // 8, second, 0)
        for q in range(tile):
            halo_start(v, q)

    def back_copy(v, r, q):
        return pltpu.make_async_remote_copy(
            src_ref=send.at[v, r, q], dst_ref=back[v][q].at[r],
            send_sem=b_send.at[v, r, q], recv_sem=b_recv.at[v, r, q],
            device_id=(view, lax.rem(own + r, n)), device_id_type=MESH)

    def finish(v, q):
        halo_wait(v, q)

        def last(c, carry):
            work[v][c * tile + q] = dot(lza[v], stacked(pad2[v][c, q], 0))
            return carry

        lax.fori_loop(0, n, last, 0, unroll=4)
        for r in range(1, n):
            send[v, r, q] = work[v][table[v, 3, r] * tile + q]
            back_copy(v, r, q).start()

    for v in range(views):
        assemble(v)
    for v in range(views):
        blur_and_ratio(v)
    has_below, has_above = view > 0, view < m - 1
    lower = 2 * view < m
    parts = up_in.shape[0] // tile
    share = n // parts
    chunks = tile * parts

    def up_copy(i):
        return pltpu.make_async_remote_copy(
            src_ref=up_out.at[i], dst_ref=up_in.at[i], send_sem=c_send.at[0, i], recv_sem=c_recv.at[0, i],
            device_id=(lax.rem(view + 1, m), own), device_id_type=MESH)

    def down_copy(i):
        return pltpu.make_async_remote_copy(
            src_ref=down_out.at[i], dst_ref=down_in.at[i], send_sem=c_send.at[1, i], recv_sem=c_recv.at[1, i],
            device_id=(lax.rem(view + m - 1, m), own), device_id_type=MESH)

    def local_product(i):
        q, part = i // parts, i % parts
        if part == 0:
            for v in range(views):
                for r in range(1, n):
                    back_copy(v, r, q).wait()
        for k in range(share):
            product = None
            for v in range(views):
                world = part * share + k
                slot = table[v, 4, world]
                value = jnp.where(slot == 0, work[v][table[v, 5, world] * tile + q], back[v][q][slot])
                product = value if product is None else product * value
            out_ref[i, k] = product

        @pl.when(view == 0)
        def _():
            up_out[i] = out_ref[i]
            up_copy(i).start()

        @pl.when(view == m - 1)
        def _():
            down_out[i] = out_ref[i]
            down_copy(i).start()

    def pass_up(i):
        @pl.when(has_below)
        def _():
            up_copy(i).wait_recv()

            @pl.when(has_above)
            def _():
                up_out[i] = up_in[i] * out_ref[i]
                up_copy(i).start()

    def pass_down(i):
        @pl.when(has_above)
        def _():
            down_copy(i).wait_recv()

            @pl.when(has_below)
            def _():
                down_out[i] = down_in[i] * out_ref[i]
                down_copy(i).start()

    def near(i):
        @pl.when(lower)
        def _():
            pass_up(i)

        @pl.when(jnp.logical_not(lower))
        def _():
            pass_down(i)

    def far(i):
        @pl.when(lower)
        def _():
            pass_down(i)

        @pl.when(jnp.logical_not(lower))
        def _():
            pass_up(i)

        @pl.when(has_below & has_above)
        def _():
            out_ref[i] = up_out[i] * down_in[i]

        @pl.when(has_below & jnp.logical_not(has_above))
        def _():
            out_ref[i] = out_ref[i] * up_in[i]

        @pl.when(has_above & jnp.logical_not(has_below))
        def _():
            out_ref[i] = out_ref[i] * down_in[i]

    ahead = min(2, tile)
    for q in range(ahead):
        for v in range(views):
            finish(v, q)
    for i in range(chunks):
        local_product(i)
        if i % parts == 0 and i // parts + ahead < tile:
            for v in range(views):
                finish(v, i // parts + ahead)
        if i >= parts:
            near(i - parts)
    for i in range(chunks - parts, chunks):
        near(i)
    for i in range(chunks):
        far(i)
    for i in range(chunks):
        @pl.when(has_above)
        def _(i=i):
            up_copy(i).wait_send()

        @pl.when(has_below)
        def _(i=i):
            down_copy(i).wait_send()


def local(n, m, estimate, recorded, psf_taps, tile_map):
    views, _, taps = psf_taps.shape
    depth, height, width = estimate.shape
    tile = height // n
    own = lax.axis_index("slab")
    count = jnp.arange(n, dtype=jnp.int32)
    flat = tile_map.reshape(views, 1, n * n)
    where_shown = (flat == (own * n + count)[None, :, None]).astype(jnp.int32)
    inverse = jnp.sum(where_shown * jnp.arange(n * n, dtype=jnp.int32), axis=2)
    shown = lax.dynamic_index_in_dim(tile_map, own, 1, keepdims=False)

    def choose(slabs):
        ahead = (slabs - own + n) % n
        hits = (ahead[:, None, :] == count[None, :, None]) & (count[None, :, None] > 0)
        return jnp.sum(hits.astype(jnp.int32) * count, axis=2)

    table = jnp.stack(
        [choose(inverse // n), (own - shown // n + n) % n, shown % n,
         choose(shown // n), (own - inverse // n + n) % n, inverse % n], axis=1)

    padded = depth + 2 * HALO
    vmem = pltpu.VMEM
    dma = pltpu.SemaphoreType.DMA
    scratch = [vmem((n, tile, depth, width), F32), vmem((views, n, tile, depth, width), F32)]
    scratch += [vmem((n, tile, depth, width), F32) for _ in range(views)]
    scratch += [vmem((height, padded, width), F32) for _ in range(views)]
    scratch += [vmem((n, tile, padded, width), F32) for _ in range(views)]
    scratch += [vmem((height, depth, width), F32) for _ in range(views)]
    scratch += [vmem((n, depth, width), F32) for _ in range(views * tile)]
    parts = PARTS if n % PARTS == 0 else 1
    chunks = tile * parts
    scratch += [vmem((chunks, n // parts, depth, width), F32) for _ in range(4)]
    scratch += [vmem((views, depth, 3 * padded), BF16) for _ in range(2)]
    scratch += [vmem((views, height, 3 * height), BF16) for _ in range(2)]
    scratch += [vmem((views, 3 * width, width), BF16) for _ in range(2)]
    scratch += [dma((views, n)), dma((views, n)), dma((views, tile + 1, 2)), dma((views, tile + 1, 2)),
                dma((views, n, tile)), dma((views, n, tile)), dma((2, chunks)), dma((2, chunks))]
    product = pl.pallas_call(
        functools.partial(kernel, n, m, views, taps),
        out_shape=jax.ShapeDtypeStruct((chunks, n // parts, depth, width), F32),
        in_specs=[pl.BlockSpec(memory_space=pltpu.SMEM)] * 2 + [pl.BlockSpec(memory_space=pltpu.VMEM)] * 2,
        out_specs=pl.BlockSpec(memory_space=pltpu.VMEM),
        scratch_shapes=scratch,
        compiler_params=pltpu.CompilerParams(
            collective_id=0, has_side_effects=True, vmem_limit_bytes=60 * 1024 * 1024),
    )(table, psf_taps, estimate, recorded)
    product = product.reshape(tile, n, depth, width)
    return estimate * product.transpose(2, 1, 0, 3).reshape(depth, height, width)


def solution(mesh):
    n, m = mesh.shape["slab"], mesh.shape["view"]
    in_specs = (
        P("slab", None, None),
        P("view", "slab", None, None),
        P("view", None, None),
        P("view", None, None),
    )
    return jax.shard_map(
        functools.partial(local, n, m), mesh=mesh, in_specs=in_specs,
        out_specs=P("slab", None, None), check_vma=False)
```

```python
import functools

import jax
import jax.numpy as jnp
from jax import lax
from jax.experimental import pallas as pl
from jax.experimental.pallas import tpu as pltpu
from jax.sharding import PartitionSpec as P

HALO = 16
PARTS = 1
MESH = pl.DeviceIdType.MESH
F32 = jnp.float32
BF16 = jnp.bfloat16


def split(value):
    high = value.astype(BF16)
    low = (value - high.astype(F32)).astype(BF16)
    return high, low


def stacked(value, axis):
    high, low = split(value)
    return jnp.concatenate([high, low, high], axis=axis)


def dot(left, right):
    return jnp.dot(left, right, preferred_element_type=F32)


def select_taps(position, tap, taps):
    total = jnp.zeros(position.shape, F32)
    for t in range(taps):
        total = jnp.where(position == t, tap(t), total)
    return total


def column_divisor(columns, tap, taps, length):
    half = taps // 2
    total = jnp.zeros(columns.shape, F32)
    for t in range(taps):
        cell = columns + (t - half)
        total = total + jnp.where((cell >= 0) & (cell < length), tap(t), 0.0)
    return total


def kernel(n, m, views, taps, *refs):
    map_ref, tap_ref, est_ref, rec_ref, out_ref = refs[:5]
    rest = list(refs[5:])
    height, depth, width = rec_ref.shape[2], rec_ref.shape[1], rec_ref.shape[3]
    tile = height // n
    padded = depth + 2 * HALO
    half = taps // 2
    view = lax.axis_index("view")
    own = lax.axis_index("slab")
    est_t = rest.pop(0)
    send = rest.pop(0)
    arrived = [rest.pop(0) for _ in range(views)]
    pad1 = [rest.pop(0) for _ in range(views)]
    pad2 = [rest.pop(0) for _ in range(views)]
    work = [rest.pop(0) for _ in range(views)]
    back = [[rest.pop(0) for _ in range(tile)] for _ in range(views)]
    up_in, up_out, down_in, down_out = [rest.pop(0) for _ in range(4)]
    lz, lza, ly, lya, rx, rxa = [rest.pop(0) for _ in range(6)]
    f_send, f_recv, h_send, h_recv, b_send, b_recv, c_send, c_recv, table = rest

    barrier = pltpu.get_barrier_semaphore()

    for v in range(views):
        pad1[v][:, 0:HALO, :] = jnp.zeros((height, HALO, width), F32)
        pad1[v][:, HALO + depth:, :] = jnp.zeros((height, HALO, width), F32)
        pad2[v][:, :, 0:HALO, :] = jnp.zeros((n, tile, HALO, width), F32)
        pad2[v][:, :, HALO + depth:, :] = jnp.zeros((n, tile, HALO, width), F32)

    for r in range(1, n):
        pl.semaphore_signal(barrier, inc=1, device_id=(view, lax.rem(own + r, n)), device_id_type=MESH)
    for r in range(1, m):
        pl.semaphore_signal(barrier, inc=1, device_id=(lax.rem(view + r, m), own), device_id_type=MESH)

    for g in range(height // 8):
        block = jnp.swapaxes(est_ref[:, g * 8:g * 8 + 8, :], 0, 1)
        if tile <= 8:
            per = 8 // tile
            est_t[g * per:(g + 1) * per] = block.reshape(per, tile, depth, width)

    pl.semaphore_wait(barrier, n - 1 + m - 1)

    def forward_copy(v, r):
        return pltpu.make_async_remote_copy(
            src_ref=send.at[v, r], dst_ref=arrived[v].at[r],
            send_sem=f_send.at[v, r], recv_sem=f_recv.at[v, r],
            device_id=(view, lax.rem(own + r, n)), device_id_type=MESH)

    step = min(8, n)

    def slab_of(world):
        return lax.div(world, jnp.int32(n))

    def bounded(index):
        return jnp.minimum(jnp.maximum(index, 0), n - 1)

    for v in range(views):
        def pick(r, carry, v=v):
            peer = lax.rem(own + r, n)

            def add(c, total):
                world = map_ref[v, peer, c]
                slab = slab_of(world)
                return total + jnp.where(slab == own, world - slab * n, 0)

            table[v, 0, r] = bounded(lax.fori_loop(0, n, add, jnp.int32(0), unroll=step))
            return carry

        lax.fori_loop(0, n, pick, 0)

    for v in range(views):
        for r in range(1, n):
            send[v, r] = est_t[bounded(table[v, 0, r])]
            forward_copy(v, r).start()

    for v in range(views):
        def fill(k, carry, v=v):
            world = map_ref[v, own, k]
            slab = slab_of(world)
            table[v, 1, k] = bounded(lax.rem(own - slab + n, n))
            table[v, 2, k] = bounded(world - slab * n)
            peer = lax.rem(own + k, n)

            def back_tile(c, total):
                return total + jnp.where(slab_of(map_ref[v, own, c]) == peer, c, 0)

            table[v, 3, k] = bounded(lax.fori_loop(0, n, back_tile, jnp.int32(0), unroll=step))

            def scan_slab(a, total):
                def scan_tile(c, total):
                    return total + jnp.where(map_ref[v, a, c] == own * n + k, a * n + c, 0)

                return lax.fori_loop(0, n, scan_tile, total, unroll=step)

            shown = lax.fori_loop(0, n, scan_slab, jnp.int32(0))
            slab = slab_of(shown)
            table[v, 4, k] = bounded(lax.rem(own - slab + n, n))
            table[v, 5, k] = bounded(shown - slab * n)
            return carry

        lax.fori_loop(0, n, fill, 0)

    for v in range(views):
        for axis in range(3):
            tap = lambda t, v=v, axis=axis: tap_ref[v, axis, t]
            if axis < 2:
                rows, cols, shift, length, start = (
                    (depth, padded, HALO, depth * n, own * depth) if axis == 0 else (height, height, 0, height, 0))
                shape = (rows, 3 * cols)
                row = start + lax.broadcasted_iota(jnp.int32, shape, 0)
                flat = lax.broadcasted_iota(jnp.int32, shape, 1)
                group = (flat >= cols).astype(jnp.int32) + (flat >= 2 * cols).astype(jnp.int32)
                col = start + flat - group * cols - shift
                inside = (col >= 0) & (col < length)
                f = jnp.where(inside, select_taps(col - row + half, tap, taps), 0.0)
                f = f / jnp.sum(jnp.where(group == 0, f, 0.0), axis=1, keepdims=True)
                div = column_divisor(col[0:8], tap, taps, length)[0:1]
                a = jnp.where(inside, select_taps(row - col + half, tap, taps), 0.0)
                a = a / jnp.where(inside[0:1], div, 1.0)
                for ref, value in (((lz, lza), (ly, lya))[axis][0], f), (((lz, lza), (ly, lya))[axis][1], a):
                    high, low = split(value)
                    ref[v] = jnp.where(group == 2, low.astype(F32), high.astype(F32)).astype(BF16)
            else:
                shape = (width, width)
                row = lax.broadcasted_iota(jnp.int32, shape, 0)
                col = lax.broadcasted_iota(jnp.int32, shape, 1)
                f = select_taps(col - row + half, tap, taps)
                f = f / jnp.sum(f, axis=1, keepdims=True)
                a = select_taps(row - col + half, tap, taps)
                a = a / column_divisor(col[0:8], tap, taps, width)[0:1]
                for ref, value in ((rx, a), (rxa, f)):
                    high, low = split(value)
                    ref[v, 0:width] = high
                    ref[v, width:2 * width] = high
                    ref[v, 2 * width:] = low

    has_low, has_high = own > 0, own < n - 1

    def halo_copies(v, q):
        if q is None:
            pad, slot = pad1[v], tile
            own_low, own_high = pad.at[:, HALO:2 * HALO, :], pad.at[:, depth:depth + HALO, :]
            far_high, far_low = pad.at[:, HALO + depth:2 * HALO + depth, :], pad.at[:, 0:HALO, :]
        else:
            pad, slot = pad2[v], q
            own_low, own_high = pad.at[:, q, HALO:2 * HALO, :], pad.at[:, q, depth:depth + HALO, :]
            far_high, far_low = pad.at[:, q, HALO + depth:2 * HALO + depth, :], pad.at[:, q, 0:HALO, :]
        low = pltpu.make_async_remote_copy(
            src_ref=own_low, dst_ref=far_high,
            send_sem=h_send.at[v, slot, 0], recv_sem=h_recv.at[v, slot, 0],
            device_id=(view, lax.rem(own + n - 1, n)), device_id_type=MESH)
        high = pltpu.make_async_remote_copy(
            src_ref=own_high, dst_ref=far_low,
            send_sem=h_send.at[v, slot, 1], recv_sem=h_recv.at[v, slot, 1],
            device_id=(view, lax.rem(own + 1, n)), device_id_type=MESH)
        return low, high

    def halo_start(v, q=None):
        low, high = halo_copies(v, q)

        @pl.when(has_low)
        def _():
            low.start()

        @pl.when(has_high)
        def _():
            high.start()

    def halo_wait(v, q=None):
        low, high = halo_copies(v, q)

        @pl.when(has_low)
        def _():
            low.wait_send()
            high.wait_recv()

        @pl.when(has_high)
        def _():
            high.wait_send()
            low.wait_recv()

    def assemble(v):
        for r in range(1, n):
            forward_copy(v, r).wait()
        for c in range(n):
            slot = bounded(table[v, 1, c])
            value = jnp.where(slot == 0, est_t[bounded(table[v, 2, c])], arrived[v][slot])
            pad1[v][c * tile:(c + 1) * tile, HALO:HALO + depth, :] = value
        halo_start(v)

    def blur_and_ratio(v):
        halo_wait(v)

        def first(g, carry):
            left, right = lz[v], rx[v]
            rows = [dot(left, stacked(pad1[v][g * 4 + k], 0)) for k in range(4)]
            value = dot(stacked(jnp.concatenate(rows, axis=0), 1), right)
            work[v][pl.ds(g * 4, 4)] = value.reshape(4, depth, width)
            return carry

        lax.fori_loop(0, height // 4, first, 0)

        def second(g, carry):
            base = pl.multiple_of(g * 8, 8)
            left, left_a, right = ly[v], lya[v], rxa[v]
            block = jnp.swapaxes(work[v][:, pl.ds(base, 8), :], 0, 1)
            rows = []
            for k in range(8):
                blurred = dot(left, stacked(block[k], 0))
                ratio = rec_ref[v, base + k] / blurred
                rows.append(dot(left_a, stacked(ratio, 0)))
            value = dot(stacked(jnp.concatenate(rows, axis=0), 1), right)
            value = jnp.swapaxes(value.reshape(8, height, width), 0, 1).reshape(n, tile, 8, width)
            pad2[v][:, :, pl.ds(pl.multiple_of(base + HALO, 8), 8), :] = value
            return carry

        lax.fori_loop(0, depth // 8, second, 0)
        for q in range(tile):
            halo_start(v, q)

    def back_copy(v, r, q):
        return pltpu.make_async_remote_copy(
            src_ref=send.at[v, r, q], dst_ref=back[v][q].at[r],
            send_sem=b_send.at[v, r, q], recv_sem=b_recv.at[v, r, q],
            device_id=(view, lax.rem(own + r, n)), device_id_type=MESH)

    def finish(v, q):
        halo_wait(v, q)

        def last(c, carry):
            work[v][c * tile + q] = dot(lza[v], stacked(pad2[v][c, q], 0))
            return carry

        lax.fori_loop(0, n, last, 0, unroll=4)
        for r in range(1, n):
            send[v, r, q] = work[v][bounded(table[v, 3, r]) * tile + q]
            back_copy(v, r, q).start()

    for v in range(views):
        assemble(v)
    for v in range(views):
        blur_and_ratio(v)
    has_below, has_above = view > 0, view < m - 1
    lower = 2 * view < m
    parts = up_in.shape[0] // tile
    share = n // parts
    chunks = tile * parts

    def up_copy(i):
        return pltpu.make_async_remote_copy(
            src_ref=up_out.at[i], dst_ref=up_in.at[i], send_sem=c_send.at[0, i], recv_sem=c_recv.at[0, i],
            device_id=(lax.rem(view + 1, m), own), device_id_type=MESH)

    def down_copy(i):
        return pltpu.make_async_remote_copy(
            src_ref=down_out.at[i], dst_ref=down_in.at[i], send_sem=c_send.at[1, i], recv_sem=c_recv.at[1, i],
            device_id=(lax.rem(view + m - 1, m), own), device_id_type=MESH)

    def local_product(i):
        q, part = i // parts, i % parts
        if part == 0:
            for v in range(views):
                for r in range(1, n):
                    back_copy(v, r, q).wait()
        for k in range(share):
            product = None
            for v in range(views):
                world = part * share + k
                slot = bounded(table[v, 4, world])
                value = jnp.where(slot == 0, work[v][bounded(table[v, 5, world]) * tile + q], back[v][q][slot])
                product = value if product is None else product * value
            out_ref[i, k] = product

        @pl.when(view == 0)
        def _():
            up_out[i] = out_ref[i]
            up_copy(i).start()

        @pl.when(view == m - 1)
        def _():
            down_out[i] = out_ref[i]
            down_copy(i).start()

    def pass_up(i):
        @pl.when(has_below)
        def _():
            up_copy(i).wait_recv()

            @pl.when(has_above)
            def _():
                up_out[i] = up_in[i] * out_ref[i]
                up_copy(i).start()

    def pass_down(i):
        @pl.when(has_above)
        def _():
            down_copy(i).wait_recv()

            @pl.when(has_below)
            def _():
                down_out[i] = down_in[i] * out_ref[i]
                down_copy(i).start()

    def near(i):
        @pl.when(lower)
        def _():
            pass_up(i)

        @pl.when(jnp.logical_not(lower))
        def _():
            pass_down(i)

    def far(i):
        @pl.when(lower)
        def _():
            pass_down(i)

        @pl.when(jnp.logical_not(lower))
        def _():
            pass_up(i)

        @pl.when(has_below & has_above)
        def _():
            out_ref[i] = up_out[i] * down_in[i]

        @pl.when(has_below & jnp.logical_not(has_above))
        def _():
            out_ref[i] = out_ref[i] * up_in[i]

        @pl.when(has_above & jnp.logical_not(has_below))
        def _():
            out_ref[i] = out_ref[i] * down_in[i]

    ahead = min(2, tile)
    for q in range(ahead):
        for v in range(views):
            finish(v, q)
    for i in range(chunks):
        local_product(i)
        if i % parts == 0 and i // parts + ahead < tile:
            for v in range(views):
                finish(v, i // parts + ahead)
        if i >= parts:
            near(i - parts)
    for i in range(chunks - parts, chunks):
        near(i)
    for i in range(chunks):
        far(i)
    for i in range(chunks):
        @pl.when(has_above)
        def _(i=i):
            up_copy(i).wait_send()

        @pl.when(has_below)
        def _(i=i):
            down_copy(i).wait_send()


def local(n, m, estimate, recorded, psf_taps, tile_map):
    views, _, taps = psf_taps.shape
    depth, height, width = estimate.shape
    tile = height // n
    padded = depth + 2 * HALO
    vmem = pltpu.VMEM
    dma = pltpu.SemaphoreType.DMA
    scratch = [vmem((n, tile, depth, width), F32), vmem((views, n, tile, depth, width), F32)]
    scratch += [vmem((n, tile, depth, width), F32) for _ in range(views)]
    scratch += [vmem((height, padded, width), F32) for _ in range(views)]
    scratch += [vmem((n, tile, padded, width), F32) for _ in range(views)]
    scratch += [vmem((height, depth, width), F32) for _ in range(views)]
    scratch += [vmem((n, depth, width), F32) for _ in range(views * tile)]
    parts = PARTS if n % PARTS == 0 else 1
    chunks = tile * parts
    scratch += [vmem((chunks, n // parts, depth, width), F32) for _ in range(4)]
    scratch += [vmem((views, depth, 3 * padded), BF16) for _ in range(2)]
    scratch += [vmem((views, height, 3 * height), BF16) for _ in range(2)]
    scratch += [vmem((views, 3 * width, width), BF16) for _ in range(2)]
    scratch += [dma((views, n)), dma((views, n)), dma((views, tile + 1, 2)), dma((views, tile + 1, 2)),
                dma((views, n, tile)), dma((views, n, tile)), dma((2, chunks)), dma((2, chunks)), pltpu.SMEM((views, 6, n), jnp.int32)]
    product = pl.pallas_call(
        functools.partial(kernel, n, m, views, taps),
        out_shape=jax.ShapeDtypeStruct((chunks, n // parts, depth, width), F32),
        in_specs=[pl.BlockSpec(memory_space=pltpu.SMEM)] * 2 + [pl.BlockSpec(memory_space=pltpu.VMEM)] * 2,
        out_specs=pl.BlockSpec(memory_space=pltpu.VMEM),
        scratch_shapes=scratch,
        compiler_params=pltpu.CompilerParams(
            collective_id=0, has_side_effects=True, vmem_limit_bytes=60 * 1024 * 1024),
    )(tile_map, psf_taps, estimate, recorded)
    product = product.reshape(tile, n, depth, width)
    return estimate * product.transpose(2, 1, 0, 3).reshape(depth, height, width)


def solution(mesh):
    n, m = mesh.shape["slab"], mesh.shape["view"]
    in_specs = (
        P("slab", None, None),
        P("view", "slab", None, None),
        P("view", None, None),
        P("view", None, None),
    )
    return jax.shard_map(
        functools.partial(local, n, m), mesh=mesh, in_specs=in_specs,
        out_specs=P("slab", None, None), check_vma=False)
```
